128 devices in a mesh: inst: 8 (over y_hi, z), tile: 16 (over y_lo, x, core).
Axes of the slice: x: 4, y: 4 (y_hi: 2, y_lo: 2; y = y_hi * 2 + y_lo), z: 4, core: 2. Of those that a mesh axis runs over, the one named last changes fastest.
Arguments:
- magnetic: float32 [8, 3, 4, 1024, 1024], P('inst', None, None, 'tile'), may hold values from -6 to 6
- velocity: float32 [8, 3, 4, 1024, 1024], P('inst', None, None, 'tile'), may hold values from -6 to 6
Outputs:
- residual: float32 [8, 3, 4, 1024, 1024], P('inst', None, None, 'tile')
The draws below stay inside these ranges and needn't reach their ends.
All inputs are finite; a program needn't handle non-finite values.
Results may differ from the reference program's by a relative error of at most 0.000055.
Values sent between devices are 32-bit elements; how exact they have to be, the bound alone decides.
A program may use at most 192 MiB of HBM per device.

```python
import jax
import jax.numpy as jnp
from jax import lax

SLAB = 4
NY = 1024
NT = 8
NX = 1024


def steps_of(own_key, dims, split, least, largest):
    factor_of = 1.0
    for dim, blocks in split:
        draws = jax.random.uniform(jax.random.fold_in(jax.random.fold_in(own_key, 6), dim), (blocks,), jnp.float32, least / len(split), largest / len(split))
        factor_of = factor_of * jnp.repeat(jnp.exp(draws), dims[dim] // blocks).reshape((-1,) + (1,) * (len(dims) - 1 - dim))
    return factor_of


def centred(own_key, extent, scale, bound, shards=(), kind=jnp.bfloat16):
    values = jax.random.normal(own_key, extent, jnp.float32) * scale
    if len(shards) > 0:
        values = steps_of(own_key, extent, shards, -0.22, 0.18) * values
    return jnp.clip(values, min=-bound, max=bound).astype(kind)


def setup_inputs(seed: int = 0) -> dict:
    key_of = jax.random.split(jax.random.key(seed), 3)
    magnetic = centred(key_of[0], (NT, 3, SLAB, NX, NY), 1.0, 6.0, ((0, 8), (3, 16)), jnp.float32)
    velocity = centred(key_of[1], (NT, 3, SLAB, NX, NY), 1.0, 6.0, ((0, 8), (3, 16)), jnp.float32)
    return {"magnetic": magnetic, "velocity": velocity}


RESIST = 0.2
TIME_DAMP = 0.5


def time_weights(inst_count):
    instance = jnp.arange(inst_count, dtype=jnp.int32)
    offset = instance[:, None] - instance[None, :]
    phase_angle = jnp.pi * offset.astype(jnp.float32) / inst_count
    parity = (1 - 2 * (jnp.abs(offset) % 2)).astype(jnp.float32)
    off_diagonal = offset != 0
    safe_sine = jnp.where(off_diagonal, jnp.sin(phase_angle), jnp.ones_like(phase_angle))
    first_part = 0.5 * parity * jnp.cos(phase_angle) / safe_sine
    second_part = -0.5 * parity / (safe_sine * safe_sine)
    second_diag = jnp.full_like(phase_angle, -(inst_count * inst_count + 2) / 12.0)
    first_mat = jnp.where(off_diagonal, first_part, jnp.zeros_like(phase_angle))
    second_mat = jnp.where(off_diagonal, second_part, second_diag)
    return first_mat - TIME_DAMP * second_mat


def deriv_axis(values, axis):
    return (jnp.roll(values, -1, axis) - jnp.roll(values, 1, axis)) * 0.5


def second_axis(values, axis):
    return jnp.roll(values, -1, axis) + jnp.roll(values, 1, axis) - 2.0 * values


def induction(inputs):
    field_b, flow_u = inputs
    emf_x = flow_u[1] * field_b[2] - flow_u[2] * field_b[1]
    emf_y = flow_u[2] * field_b[0] - flow_u[0] * field_b[2]
    emf_z = flow_u[0] * field_b[1] - flow_u[1] * field_b[0]
    curl_terms = jnp.stack([
        deriv_axis(emf_z, 2) - deriv_axis(emf_y, 0),
        deriv_axis(emf_x, 0) - deriv_axis(emf_z, 1),
        deriv_axis(emf_y, 1) - deriv_axis(emf_x, 2)])
    laplace = second_axis(field_b, 1) + second_axis(field_b, 2) + second_axis(field_b, 3)
    return curl_terms + RESIST * laplace


def reference(magnetic, velocity):
    matrix = time_weights(NT)
    induced = lax.map(induction, (magnetic, velocity))
    derivative = jnp.einsum("nm,mczxy->nczxy", matrix, magnetic, precision=lax.Precision.HIGHEST)
    return derivative - induced
```

```python
import jax
import jax.numpy as jnp
from jax import lax
from jax.sharding import PartitionSpec as P

RESIST = 0.2
TIME_DAMP = 0.5


def with_halo(cells, sides, width):
    for axis, dim in sides:
        count = lax.axis_size(axis)
        head = lax.slice_in_dim(cells, 0, width, axis=dim)
        tail = lax.slice_in_dim(cells, cells.shape[dim] - width, cells.shape[dim], axis=dim)
        cells = jnp.concatenate(
            [
                lax.ppermute(tail, axis, [(i, (i + 1) % count) for i in range(count)]),
                cells,
                lax.ppermute(head, axis, [((i + 1) % count, i) for i in range(count)]),
            ],
            axis=dim,
        )
    return cells


def time_weights(inst_count):
    instance = jnp.arange(inst_count, dtype=jnp.int32)
    offset = instance[:, None] - instance[None, :]
    phase_angle = jnp.pi * offset.astype(jnp.float32) / inst_count
    parity = (1 - 2 * (jnp.abs(offset) % 2)).astype(jnp.float32)
    off_diagonal = offset != 0
    safe_sine = jnp.where(off_diagonal, jnp.sin(phase_angle), jnp.ones_like(phase_angle))
    first_part = 0.5 * parity * jnp.cos(phase_angle) / safe_sine
    second_part = -0.5 * parity / (safe_sine * safe_sine)
    second_diag = jnp.full_like(phase_angle, -(inst_count * inst_count + 2) / 12.0)
    first_mat = jnp.where(off_diagonal, first_part, jnp.zeros_like(phase_angle))
    second_mat = jnp.where(off_diagonal, second_part, second_diag)
    return first_mat - TIME_DAMP * second_mat


def deriv_axis(values, axis):
    return (jnp.roll(values, -1, axis) - jnp.roll(values, 1, axis)) * 0.5


def second_axis(values, axis):
    return jnp.roll(values, -1, axis) + jnp.roll(values, 1, axis) - 2.0 * values


def induction(field_b, flow_u):
    emf_x = flow_u[1] * field_b[2] - flow_u[2] * field_b[1]
    emf_y = flow_u[2] * field_b[0] - flow_u[0] * field_b[2]
    emf_z = flow_u[0] * field_b[1] - flow_u[1] * field_b[0]
    stacked = jnp.concatenate([jnp.stack([emf_x, emf_y, emf_z]), field_b], axis=0)
    extended = with_halo(stacked, (("tile", 2),), 1)
    forward_cells = extended[:, :, 2:, :]
    backward_cells = extended[:, :, :-2, :]
    x_deriv = (forward_cells - backward_cells) * 0.5
    curl_terms = jnp.stack(
        [
            deriv_axis(emf_z, 2) - deriv_axis(emf_y, 0),
            deriv_axis(emf_x, 0) - x_deriv[2],
            x_deriv[1] - deriv_axis(emf_x, 2),
        ]
    )
    x_second = forward_cells[3:] + backward_cells[3:] - 2.0 * field_b
    laplace = second_axis(field_b, 1) + x_second + second_axis(field_b, 3)
    return curl_terms + RESIST * laplace


def per_device(magnetic, velocity):
    inst_count = lax.axis_size("inst")
    matrix = time_weights(inst_count)
    induced = induction(magnetic[0], velocity[0])
    comps, planes, rows, lanes = induced.shape
    part = rows // inst_count
    pieces = magnetic[0].reshape(comps, planes, inst_count, part, lanes)
    gathered = lax.all_to_all(pieces, "inst", 2, 0, tiled=False)
    mixed = jnp.einsum("nm,mczxy->nczxy", matrix, gathered, precision=lax.Precision.HIGHEST)
    derivative = lax.all_to_all(mixed, "inst", 0, 2, tiled=False)
    return (derivative.reshape(induced.shape) - induced)[None]


def solution(mesh):
    in_specs = (P("inst", None, None, "tile", None), P("inst", None, None, "tile", None))
    out_specs = P("inst", None, None, "tile", None)
    return jax.shard_map(
        per_device, mesh=mesh, in_specs=in_specs, out_specs=out_specs, check_vma=False
    )
```

```python
import functools

import jax
import jax.numpy as jnp
import numpy as np
from jax import lax
from jax.experimental import pallas as pl
from jax.experimental.pallas import tpu as pltpu
from jax.sharding import PartitionSpec as P

RESIST = 0.2
TIME_DAMP = 0.5
LANES = 256
MESH = pl.DeviceIdType.MESH


def time_weights(count):
    k = np.arange(1, count)
    parity = np.where(k % 2 == 0, 1.0, -1.0)
    sine, cosine = np.sin(np.pi * k / count), np.cos(np.pi * k / count)
    off = 0.5 * parity * cosine / sine + TIME_DAMP * 0.5 * parity / (sine * sine)
    return [TIME_DAMP * (count * count + 2) / 12.0] + [float(v) for v in off]


def mix(fields, weights):
    count = len(fields)
    half = count // 2
    sums = [fields[k] + fields[k + half] for k in range(half)]
    diffs = [fields[k] - fields[k + half] for k in range(half)]

    def dot(terms, row):
        total = None
        for term, weight in zip(terms, row):
            part = term * np.float32(weight)
            total = part if total is None else total + part
        return total

    low, high = [], []
    for q in range(half):
        row = [weights[(q + k) % count] for k in range(half)]
        far = [weights[(q + k + half) % count] for k in range(half)]
        even = dot(sums, [(a + b) / 2 for a, b in zip(row, far)])
        odd = dot(diffs, [(a - b) / 2 for a, b in zip(row, far)])
        low.append(even + odd)
        high.append(even - odd)
    return low + high


def cross(u, b):
    return [u[1] * b[2] - u[2] * b[1], u[2] * b[0] - u[0] * b[2], u[0] * b[1] - u[1] * b[0]]


def x_terms(b, e, sign):
    half = np.float32(0.5 * sign)
    rate = np.float32(RESIST)
    return [rate * b[0], rate * b[1] - half * e[2], rate * b[2] + half * e[1]]


def kernel(weights, b_hbm, u_hbm, mixed, induced, field, flow, emf, got, out, edge, halo,
           load_sem, edge_send, edge_recv, there_send, there_recv, back_send, back_recv):
    count = len(weights)
    comps, planes, rows, lanes = field.shape
    part = rows // count
    me, tile = lax.axis_index("inst"), lax.axis_index("tile")
    tiles = lax.axis_size("tile")
    peers = [lax.rem(me + k, count) for k in range(count)]
    after, before = lax.rem(tile + 1, tiles), lax.rem(tile + tiles - 1, tiles)

    barrier = pltpu.get_barrier_semaphore()
    for k in range(1, count):
        pl.semaphore_signal(barrier, inc=1, device_id=(peers[k], tile), device_id_type=MESH)
    for other in (before, after):
        pl.semaphore_signal(barrier, inc=1, device_id=(me, other), device_id_type=MESH)

    loads = [pltpu.make_async_copy(b_hbm, field, load_sem.at[0]), pltpu.make_async_copy(u_hbm, flow, load_sem.at[1])]
    for load in loads:
        load.start()
    for load in loads:
        load.wait()

    for side, (first, row, sign) in enumerate(((0, 0, 1), (rows - 8, 7, -1))):
        for z in range(planes):
            b = [field[c, z, first:first + 8, :] for c in range(comps)]
            e = cross([flow[c, z, first:first + 8, :] for c in range(comps)], b)
            for c, term in enumerate(x_terms(b, e, sign)):
                at = c * planes + z
                edge[side, at:at + 1, :] = term[row:row + 1, :]

    pl.semaphore_wait(barrier, count + 1)

    def edge_copy(side, other):
        return pltpu.make_async_remote_copy(
            src_ref=edge.at[side], dst_ref=halo.at[side], send_sem=edge_send.at[side], recv_sem=edge_recv.at[side],
            device_id=(me, other), device_id_type=MESH)

    edges = [edge_copy(0, before), edge_copy(1, after)]
    for copy in edges:
        copy.start()

    def there(z, k):
        return pltpu.make_async_remote_copy(
            src_ref=field.at[:, z, pl.ds(pl.multiple_of(peers[k] * part, part), part), :], dst_ref=got.at[k - 1, z],
            send_sem=there_send.at[z, k - 1], recv_sem=there_recv.at[z, k - 1],
            device_id=(peers[k], tile), device_id_type=MESH)

    own = pl.ds(pl.multiple_of(me * part, part), part)

    def back(z, k):
        return pltpu.make_async_remote_copy(
            src_ref=out.at[k - 1, z], dst_ref=mixed.at[:, z, own, :],
            send_sem=back_send.at[z, k - 1], recv_sem=back_recv.at[z, k - 1],
            device_id=(peers[k], tile), device_id_type=MESH)

    for z in range(planes):
        for k in range(1, count):
            there(z, k).start()

    def emf_plane(z, carry):
        b = [field[c, z] for c in range(comps)]
        for c, value in enumerate(cross([flow[c, z] for c in range(comps)], b)):
            emf[c, z] = value
        return carry

    lax.fori_loop(0, planes, emf_plane, 0)

    for copy in edges:
        copy.wait()

    rate, half = np.float32(RESIST), np.float32(0.5)

    def induction_plane(z, carry):
        up, down = lax.rem(z + 1, planes), lax.rem(z + planes - 1, planes)
        b = [field[c, z] for c in range(comps)]
        e = [emf[c, z] for c in range(comps)]
        place = lax.broadcasted_iota(jnp.int32, (rows, lanes), 0)
        from_after, from_before = x_terms(b, e, 1), x_terms(b, e, -1)
        z_emf = [lambda at: -emf[1, at], lambda at: emf[0, at], lambda at: None]
        y_emf = [e[2], None, -e[0]]
        for c in range(comps):
            total = np.float32(-6.0 * RESIST) * b[c]
            total += rate * (field[c, up] + field[c, down])
            if c < 2:
                total += half * (z_emf[c](up) - z_emf[c](down))
            diffusive = rate * b[c]
            ahead, behind = diffusive, diffusive
            if y_emf[c] is not None:
                ahead, behind = diffusive + half * y_emf[c], diffusive - half * y_emf[c]
            total += pltpu.roll(ahead, lanes - 1, 1) + pltpu.roll(behind, 1, 1)
            row = c * planes + z
            next_row, last_row = halo[0, pl.ds(row, 1), :], halo[1, pl.ds(row, 1), :]
            total += jnp.where(place == rows - 1, next_row, pltpu.roll(from_after[c], rows - 1, 0))
            total += jnp.where(place == 0, last_row, pltpu.roll(from_before[c], 1, 0))
            induced[c, z] = total
        return carry

    lax.fori_loop(0, planes, induction_plane, 0)

    steps = lanes // LANES
    for z in range(planes):
        for k in range(1, count):
            there(z, k).wait_recv()

        def mix_block(i, carry, z=z):
            c, at = i // steps, pl.ds(pl.multiple_of((i % steps) * LANES, LANES), LANES)
            fields = [field[c, z, own, at]] + [got[k, z, c, :, at] for k in range(count - 1)]
            values = mix(fields, weights)
            mixed[c, z, own, at] = values[0]
            for k in range(1, count):
                out[k - 1, z, c, :, at] = values[k]
            return carry

        lax.fori_loop(0, comps * steps, mix_block, 0)
        for k in range(1, count):
            back(z, k).start()

    for z in range(planes):
        for k in range(1, count):
            there(z, k).wait_send()
            back(z, k).wait()


def per_device(magnetic, velocity):
    inst_count = lax.axis_size("inst")
    field, flow = (pltpu.with_memory_space_constraint(a[0], pltpu.HBM) for a in (magnetic, velocity))
    shape = field.shape
    comps, planes, rows, lanes = shape
    part = rows // inst_count
    vmem = pl.BlockSpec(memory_space=pltpu.VMEM)
    block = jax.ShapeDtypeStruct(shape, jnp.float32)
    mixed, induced = pl.pallas_call(
        functools.partial(kernel, time_weights(inst_count)),
        out_shape=(block, block),
        in_specs=[pl.BlockSpec(memory_space=pltpu.HBM)] * 2,
        out_specs=(vmem, vmem),
        scratch_shapes=[
            pltpu.VMEM(shape, jnp.float32),
            pltpu.VMEM(shape, jnp.float32),
            pltpu.VMEM(shape, jnp.float32),
            pltpu.VMEM((inst_count - 1, planes, comps, part, lanes), jnp.float32),
            pltpu.VMEM((inst_count - 1, planes, comps, part, lanes), jnp.float32),
            pltpu.VMEM((2, comps * planes, lanes), jnp.float32),
            pltpu.VMEM((2, comps * planes, lanes), jnp.float32),
            pltpu.SemaphoreType.DMA((2,)),
            pltpu.SemaphoreType.DMA((2,)),
            pltpu.SemaphoreType.DMA((2,)),
            pltpu.SemaphoreType.DMA((planes, inst_count - 1)),
            pltpu.SemaphoreType.DMA((planes, inst_count - 1)),
            pltpu.SemaphoreType.DMA((planes, inst_count - 1)),
            pltpu.SemaphoreType.DMA((planes, inst_count - 1)),
        ],
        compiler_params=pltpu.CompilerParams(
            collective_id=0, has_side_effects=True, vmem_limit_bytes=40 * 2**20
        ),
    )(field, flow)
    return (mixed - induced)[None]


def solution(mesh):
    in_specs = (P("inst", None, None, "tile", None), P("inst", None, None, "tile", None))
    out_specs = P("inst", None, None, "tile", None)
    return jax.shard_map(
        per_device, mesh=mesh, in_specs=in_specs, out_specs=out_specs, check_vma=False
    )
```

```python
import functools

import jax
import jax.numpy as jnp
import numpy as np
from jax import lax
from jax.experimental import pallas as pl
from jax.experimental.pallas import tpu as pltpu
from jax.sharding import PartitionSpec as P

RESIST = 0.2
TIME_DAMP = 0.5
LANES = 256
RING = 4
NEAR = ((0, 1), (0, -1), (0, 2), (1, 0))
FAR = ((1, 1), (1, -1), (1, 2))
STEPS = NEAR + FAR
ACROSS = (1, 0)
MESH = pl.DeviceIdType.MESH


def time_weights(count):
    k = np.arange(1, count)
    parity = np.where(k % 2 == 0, 1.0, -1.0)
    sine, cosine = np.sin(np.pi * k / count), np.cos(np.pi * k / count)
    off = 0.5 * parity * cosine / sine + TIME_DAMP * 0.5 * parity / (sine * sine)
    return [TIME_DAMP * (count * count + 2) / 12.0] + [float(v) for v in off]


def mix(fields, weights):
    count = len(fields)
    half = count // 2
    sums = [fields[k] + fields[k + half] for k in range(half)]
    diffs = [fields[k] - fields[k + half] for k in range(half)]

    def dot(terms, row):
        total = None
        for term, weight in zip(terms, row):
            part = term * np.float32(weight)
            total = part if total is None else total + part
        return total

    low, high = [], []
    for q in range(half):
        row = [weights[(q + k) % count] for k in range(half)]
        far = [weights[(q + k + half) % count] for k in range(half)]
        even = dot(sums, [(a + b) / 2 for a, b in zip(row, far)])
        odd = dot(diffs, [(a - b) / 2 for a, b in zip(row, far)])
        low.append(even + odd)
        high.append(even - odd)
    return low + high


def cross(u, b):
    return [u[1] * b[2] - u[2] * b[1], u[2] * b[0] - u[0] * b[2], u[0] * b[1] - u[1] * b[0]]


def x_terms(b, e, sign):
    half = np.float32(0.5 * sign)
    rate = np.float32(RESIST)
    return [rate * b[0], rate * b[1] - half * e[2], rate * b[2] + half * e[1]]


def kernel(weights, b_hbm, u_hbm, mixed, induced, field, flow, emf, got, out, edge, halo,
           load_sem, edge_send, edge_recv, there_send, there_recv, back_send, back_recv, ready):
    count = len(weights)
    comps, planes, rows, lanes = field.shape
    part = rows // count
    me, tile = lax.axis_index("inst"), lax.axis_index("tile")
    tiles = lax.axis_size("tile")
    after, before = lax.rem(tile + 1, tiles), lax.rem(tile + tiles - 1, tiles)

    def moved(step):
        return lax.rem(me // RING + step[0], 2) * RING + lax.rem(me % RING + step[1] + RING, RING)

    def slot(step):
        return lax.rem(moved(step) - me + count, count) - 1

    barrier = pltpu.get_barrier_semaphore()
    for step in NEAR:
        pl.semaphore_signal(barrier, inc=1, device_id=(moved(step), tile), device_id_type=MESH)
    for other in (before, after):
        pl.semaphore_signal(barrier, inc=1, device_id=(me, other), device_id_type=MESH)

    loads = [pltpu.make_async_copy(b_hbm, field, load_sem.at[0]), pltpu.make_async_copy(u_hbm, flow, load_sem.at[1])]
    for load in loads:
        load.start()
    pl.semaphore_wait(barrier, len(NEAR) + 2)
    pl.semaphore_signal(ready, inc=1, device_id=(moved(ACROSS), tile), device_id_type=MESH)

    def there(z, p):
        step = STEPS[p]
        return pltpu.make_async_remote_copy(
            src_ref=b_hbm.at[:, z, pl.ds(pl.multiple_of(moved(step) * part, part), part), :], dst_ref=got.at[slot(step), z],
            send_sem=there_send.at[z, p], recv_sem=there_recv.at[z, p],
            device_id=(moved(step), tile), device_id_type=MESH)

    own = pl.ds(pl.multiple_of(me * part, part), part)

    def back(z, p):
        step = STEPS[p]
        return pltpu.make_async_remote_copy(
            src_ref=out.at[slot(step), z], dst_ref=mixed.at[:, z, own, :],
            send_sem=back_send.at[z, p], recv_sem=back_recv.at[z, p],
            device_id=(moved(step), tile), device_id_type=MESH)

    near, far = range(len(NEAR)), range(len(NEAR), len(STEPS))
    for z in range(2):
        for p in near:
            there(z, p).start()
    pl.semaphore_wait(ready, 1)
    for z in range(2):
        for p in far:
            there(z, p).start()
    for z in range(2, planes):
        for p in range(len(STEPS)):
            there(z, p).start()

    for load in loads:
        load.wait()

    for side, (first, row, sign) in enumerate(((0, 0, 1), (rows - 8, 7, -1))):
        for z in range(planes):
            b = [field[c, z, first:first + 8, :] for c in range(comps)]
            e = cross([flow[c, z, first:first + 8, :] for c in range(comps)], b)
            for c, term in enumerate(x_terms(b, e, sign)):
                at = c * planes + z
                edge[side, at:at + 1, :] = term[row:row + 1, :]

    def edge_copy(side, other):
        return pltpu.make_async_remote_copy(
            src_ref=edge.at[side], dst_ref=halo.at[side], send_sem=edge_send.at[side], recv_sem=edge_recv.at[side],
            device_id=(me, other), device_id_type=MESH)

    edges = [edge_copy(0, before), edge_copy(1, after)]
    for copy in edges:
        copy.start()

    def emf_plane(z, carry):
        b = [field[c, z] for c in range(comps)]
        for c, value in enumerate(cross([flow[c, z] for c in range(comps)], b)):
            emf[c, z] = value
        return carry

    steps = lanes // LANES
    for z in range(planes):
        for p in range(len(STEPS)):
            there(z, p).wait_recv()

        def mix_block(i, carry, z=z):
            c, at = i // steps, pl.ds(pl.multiple_of((i % steps) * LANES, LANES), LANES)
            fields = [field[c, z, own, at]] + [got[k, z, c, :, at] for k in range(count - 1)]
            values = mix(fields, weights)
            mixed[c, z, own, at] = values[0]
            for k in range(1, count):
                out[k - 1, z, c, :, at] = values[k]
            return carry

        lax.fori_loop(0, comps * steps, mix_block, 0)
        for p in range(len(STEPS)):
            back(z, p).start()

    lax.fori_loop(0, planes, emf_plane, 0)

    for copy in edges:
        copy.wait()

    rate, half = np.float32(RESIST), np.float32(0.5)

    def induction_plane(z, carry):
        up, down = lax.rem(z + 1, planes), lax.rem(z + planes - 1, planes)
        b = [field[c, z] for c in range(comps)]
        e = [emf[c, z] for c in range(comps)]
        place = lax.broadcasted_iota(jnp.int32, (rows, lanes), 0)
        from_after, from_before = x_terms(b, e, 1), x_terms(b, e, -1)
        z_emf = [lambda at: -emf[1, at], lambda at: emf[0, at], lambda at: None]
        y_emf = [e[2], None, -e[0]]
        for c in range(comps):
            total = np.float32(-6.0 * RESIST) * b[c]
            total += rate * (field[c, up] + field[c, down])
            if c < 2:
                total += half * (z_emf[c](up) - z_emf[c](down))
            diffusive = rate * b[c]
            ahead, behind = diffusive, diffusive
            if y_emf[c] is not None:
                ahead, behind = diffusive + half * y_emf[c], diffusive - half * y_emf[c]
            total += pltpu.roll(ahead, lanes - 1, 1) + pltpu.roll(behind, 1, 1)
            row = c * planes + z
            next_row, last_row = halo[0, pl.ds(row, 1), :], halo[1, pl.ds(row, 1), :]
            total += jnp.where(place == rows - 1, next_row, pltpu.roll(from_after[c], rows - 1, 0))
            total += jnp.where(place == 0, last_row, pltpu.roll(from_before[c], 1, 0))
            induced[c, z] = total
        return carry

    lax.fori_loop(0, planes, induction_plane, 0)

    for z in range(planes):
        for p in range(len(STEPS)):
            there(z, p).wait_send()
            back(z, p).wait()


def finish(mixed, induced, result, block, sem):
    copies = [pltpu.make_async_copy(block.at[i], result.at[i], sem.at[i]) for i in range(block.shape[0])]
    for i, copy in enumerate(copies):
        block[i] = mixed[i] - induced[i]
        copy.start()
    for copy in copies:
        copy.wait()


def per_device(magnetic, velocity):
    inst_count = lax.axis_size("inst")
    field, flow = (pltpu.with_memory_space_constraint(a[0], pltpu.HBM) for a in (magnetic, velocity))
    shape = field.shape
    comps, planes, rows, lanes = shape
    part = rows // inst_count
    vmem = pl.BlockSpec(memory_space=pltpu.VMEM)
    block = jax.ShapeDtypeStruct(shape, jnp.float32)
    mixed, induced = pl.pallas_call(
        functools.partial(kernel, time_weights(inst_count)),
        out_shape=(block, block),
        in_specs=[pl.BlockSpec(memory_space=pltpu.HBM)] * 2,
        out_specs=(vmem, vmem),
        scratch_shapes=[
            pltpu.VMEM(shape, jnp.float32),
            pltpu.VMEM(shape, jnp.float32),
            pltpu.VMEM(shape, jnp.float32),
            pltpu.VMEM((inst_count - 1, planes, comps, part, lanes), jnp.float32),
            pltpu.VMEM((inst_count - 1, planes, comps, part, lanes), jnp.float32),
            pltpu.VMEM((2, comps * planes, lanes), jnp.float32),
            pltpu.VMEM((2, comps * planes, lanes), jnp.float32),
            pltpu.SemaphoreType.DMA((2,)),
            pltpu.SemaphoreType.DMA((2,)),
            pltpu.SemaphoreType.DMA((2,)),
            pltpu.SemaphoreType.DMA((planes, inst_count - 1)),
            pltpu.SemaphoreType.DMA((planes, inst_count - 1)),
            pltpu.SemaphoreType.DMA((planes, inst_count - 1)),
            pltpu.SemaphoreType.DMA((planes, inst_count - 1)),
            pltpu.SemaphoreType.REGULAR,
        ],
        compiler_params=pltpu.CompilerParams(
            collective_id=0, has_side_effects=True, vmem_limit_bytes=40 * 2**20
        ),
    )(field, flow)
    flat = (comps * planes, rows, lanes)
    result = pl.pallas_call(
        finish,
        out_shape=jax.ShapeDtypeStruct(flat, jnp.float32),
        in_specs=[vmem, vmem],
        out_specs=pl.BlockSpec(memory_space=pltpu.HBM),
        scratch_shapes=[pltpu.VMEM(flat, jnp.float32), pltpu.SemaphoreType.DMA((comps * planes,))],
        compiler_params=pltpu.CompilerParams(vmem_limit_bytes=40 * 2**20),
    )(mixed.reshape(flat), induced.reshape(flat))
    return result.reshape((1,) + shape)


def solution(mesh):
    in_specs = (P("inst", None, None, "tile", None), P("inst", None, None, "tile", None))
    out_specs = P("inst", None, None, "tile", None)
    return jax.shard_map(
        per_device, mesh=mesh, in_specs=in_specs, out_specs=out_specs, check_vma=False
    )
```

```python
import functools

import jax
import jax.numpy as jnp
import numpy as np
from jax import lax
from jax.experimental import pallas as pl
from jax.experimental.pallas import tpu as pltpu
from jax.sharding import PartitionSpec as P

RESIST = 0.2
TIME_DAMP = 0.5
LANES = 256
RING = 4
STEPS = ((1, 0), (1, 1), (1, -1), (1, 2), (0, 1), (0, -1), (0, 2))
LAST = (3, 1, 2, 0, 6, 4, 5)
MESH = pl.DeviceIdType.MESH


def time_weights(count):
    k = np.arange(1, count)
    parity = np.where(k % 2 == 0, 1.0, -1.0)
    sine, cosine = np.sin(np.pi * k / count), np.cos(np.pi * k / count)
    off = 0.5 * parity * cosine / sine + TIME_DAMP * 0.5 * parity / (sine * sine)
    return [TIME_DAMP * (count * count + 2) / 12.0] + [float(v) for v in off]


def mix(fields, weights):
    count = len(fields)
    half = count // 2
    sums = [fields[k] + fields[k + half] for k in range(half)]
    diffs = [fields[k] - fields[k + half] for k in range(half)]

    def dot(terms, row):
        total = None
        for term, weight in zip(terms, row):
            part = term * np.float32(weight)
            total = part if total is None else total + part
        return total

    low, high = [], []
    for q in range(half):
        row = [weights[(q + k) % count] for k in range(half)]
        far = [weights[(q + k + half) % count] for k in range(half)]
        even = dot(sums, [(a + b) / 2 for a, b in zip(row, far)])
        odd = dot(diffs, [(a - b) / 2 for a, b in zip(row, far)])
        low.append(even + odd)
        high.append(even - odd)
    return low + high


def cross(u, b):
    return [u[1] * b[2] - u[2] * b[1], u[2] * b[0] - u[0] * b[2], u[0] * b[1] - u[1] * b[0]]


def x_terms(b, e, sign):
    half = np.float32(0.5 * sign)
    rate = np.float32(RESIST)
    return [rate * b[0], rate * b[1] - half * e[2], rate * b[2] + half * e[1]]


def kernel(weights, b_hbm, u_hbm, mixed, induced, field, flow, emf, got, out, edge, halo,
           load_sem, edge_send, edge_recv, there_send, there_recv, back_send, back_recv):
    count = len(weights)
    comps, planes, rows, lanes = field.shape
    part = rows // count
    me, tile = lax.axis_index("inst"), lax.axis_index("tile")
    tiles = lax.axis_size("tile")
    after, before = lax.rem(tile + 1, tiles), lax.rem(tile + tiles - 1, tiles)

    def moved(step):
        return lax.rem(me // RING + step[0], 2) * RING + lax.rem(me % RING + step[1] + RING, RING)

    def slot(step):
        return lax.rem(moved(step) - me + count, count) - 1

    barrier = pltpu.get_barrier_semaphore()
    for step in STEPS:
        pl.semaphore_signal(barrier, inc=1, device_id=(moved(step), tile), device_id_type=MESH)
    for other in (before, after):
        pl.semaphore_signal(barrier, inc=1, device_id=(me, other), device_id_type=MESH)

    loads = [pltpu.make_async_copy(b_hbm, field, load_sem.at[0]), pltpu.make_async_copy(u_hbm, flow, load_sem.at[1])]
    pl.semaphore_wait(barrier, len(STEPS) + 2)

    def there(z, p):
        step = STEPS[p]
        return pltpu.make_async_remote_copy(
            src_ref=b_hbm.at[:, z, pl.ds(pl.multiple_of(moved(step) * part, part), part), :], dst_ref=got.at[slot(step), z],
            send_sem=there_send.at[z, p], recv_sem=there_recv.at[z, p],
            device_id=(moved(step), tile), device_id_type=MESH)

    own = pl.ds(pl.multiple_of(me * part, part), part)

    def back(z, p):
        step = STEPS[p]
        return pltpu.make_async_remote_copy(
            src_ref=out.at[slot(step), z], dst_ref=mixed.at[:, z, own, :],
            send_sem=back_send.at[z, p], recv_sem=back_recv.at[z, p],
            device_id=(moved(step), tile), device_id_type=MESH)

    for z in range(planes):
        for p in range(len(STEPS)):
            there(z, p).start()

    for load in loads:
        load.start()
    for load in loads:
        load.wait()

    for side, (first, row, sign) in enumerate(((0, 0, 1), (rows - 8, 7, -1))):
        for z in range(planes):
            b = [field[c, z, first:first + 8, :] for c in range(comps)]
            e = cross([flow[c, z, first:first + 8, :] for c in range(comps)], b)
            for c, term in enumerate(x_terms(b, e, sign)):
                at = c * planes + z
                edge[side, at:at + 1, :] = term[row:row + 1, :]

    def edge_copy(side, other):
        return pltpu.make_async_remote_copy(
            src_ref=edge.at[side], dst_ref=halo.at[side], send_sem=edge_send.at[side], recv_sem=edge_recv.at[side],
            device_id=(me, other), device_id_type=MESH)

    edges = [edge_copy(0, before), edge_copy(1, after)]
    for copy in edges:
        copy.start()

    def emf_plane(z, carry):
        b = [field[c, z] for c in range(comps)]
        for c, value in enumerate(cross([flow[c, z] for c in range(comps)], b)):
            emf[c, z] = value
        return carry

    steps = lanes // LANES
    for z in range(planes):
        for p in range(len(STEPS)):
            there(z, p).wait_recv()

        def mix_block(i, carry, z=z):
            c, at = i // steps, pl.ds(pl.multiple_of((i % steps) * LANES, LANES), LANES)
            fields = [field[c, z, own, at]] + [got[k, z, c, :, at] for k in range(count - 1)]
            values = mix(fields, weights)
            mixed[c, z, own, at] = values[0]
            for k in range(1, count):
                out[k - 1, z, c, :, at] = values[k]
            return carry

        lax.fori_loop(0, comps * steps, mix_block, 0)
        for p in LAST if z == planes - 1 else range(len(STEPS)):
            back(z, p).start()

    lax.fori_loop(0, planes, emf_plane, 0)

    for copy in edges:
        copy.wait()

    rate, half = np.float32(RESIST), np.float32(0.5)

    def induction_plane(z, carry):
        up, down = lax.rem(z + 1, planes), lax.rem(z + planes - 1, planes)
        b = [field[c, z] for c in range(comps)]
        e = [emf[c, z] for c in range(comps)]
        place = lax.broadcasted_iota(jnp.int32, (rows, lanes), 0)
        from_after, from_before = x_terms(b, e, 1), x_terms(b, e, -1)
        z_emf = [lambda at: -emf[1, at], lambda at: emf[0, at], lambda at: None]
        y_emf = [e[2], None, -e[0]]
        for c in range(comps):
            total = np.float32(-6.0 * RESIST) * b[c]
            total += rate * (field[c, up] + field[c, down])
            if c < 2:
                total += half * (z_emf[c](up) - z_emf[c](down))
            diffusive = rate * b[c]
            ahead, behind = diffusive, diffusive
            if y_emf[c] is not None:
                ahead, behind = diffusive + half * y_emf[c], diffusive - half * y_emf[c]
            total += pltpu.roll(ahead, lanes - 1, 1) + pltpu.roll(behind, 1, 1)
            row = c * planes + z
            next_row, last_row = halo[0, pl.ds(row, 1), :], halo[1, pl.ds(row, 1), :]
            total += jnp.where(place == rows - 1, next_row, pltpu.roll(from_after[c], rows - 1, 0))
            total += jnp.where(place == 0, last_row, pltpu.roll(from_before[c], 1, 0))
            induced[c, z] = total
        return carry

    lax.fori_loop(0, planes, induction_plane, 0)

    for z in range(planes):
        for p in range(len(STEPS)):
            there(z, p).wait_send()
            back(z, p).wait()


def finish(mixed, induced, result, block, sem):
    copies = [pltpu.make_async_copy(block.at[i], result.at[i], sem.at[i]) for i in range(block.shape[0])]
    for i, copy in enumerate(copies):
        block[i] = mixed[i] - induced[i]
        copy.start()
    for copy in copies:
        copy.wait()


def per_device(magnetic, velocity):
    inst_count = lax.axis_size("inst")
    field, flow = (pltpu.with_memory_space_constraint(a[0], pltpu.HBM) for a in (magnetic, velocity))
    shape = field.shape
    comps, planes, rows, lanes = shape
    part = rows // inst_count
    vmem = pl.BlockSpec(memory_space=pltpu.VMEM)
    block = jax.ShapeDtypeStruct(shape, jnp.float32)
    mixed, induced = pl.pallas_call(
        functools.partial(kernel, time_weights(inst_count)),
        out_shape=(block, block),
        in_specs=[pl.BlockSpec(memory_space=pltpu.HBM)] * 2,
        out_specs=(vmem, vmem),
        scratch_shapes=[
            pltpu.VMEM(shape, jnp.float32),
            pltpu.VMEM(shape, jnp.float32),
            pltpu.VMEM(shape, jnp.float32),
            pltpu.VMEM((inst_count - 1, planes, comps, part, lanes), jnp.float32),
            pltpu.VMEM((inst_count - 1, planes, comps, part, lanes), jnp.float32),
            pltpu.VMEM((2, comps * planes, lanes), jnp.float32),
            pltpu.VMEM((2, comps * planes, lanes), jnp.float32),
            pltpu.SemaphoreType.DMA((2,)),
            pltpu.SemaphoreType.DMA((2,)),
            pltpu.SemaphoreType.DMA((2,)),
            pltpu.SemaphoreType.DMA((planes, inst_count - 1)),
            pltpu.SemaphoreType.DMA((planes, inst_count - 1)),
            pltpu.SemaphoreType.DMA((planes, inst_count - 1)),
            pltpu.SemaphoreType.DMA((planes, inst_count - 1)),
        ],
        compiler_params=pltpu.CompilerParams(
            collective_id=0, has_side_effects=True, vmem_limit_bytes=40 * 2**20
        ),
    )(field, flow)
    flat = (comps * planes, rows, lanes)
    result = pl.pallas_call(
        finish,
        out_shape=jax.ShapeDtypeStruct(flat, jnp.float32),
        in_specs=[vmem, vmem],
        out_specs=pl.BlockSpec(memory_space=pltpu.HBM),
        scratch_shapes=[pltpu.VMEM(flat, jnp.float32), pltpu.SemaphoreType.DMA((comps * planes,))],
        compiler_params=pltpu.CompilerParams(vmem_limit_bytes=40 * 2**20),
    )(mixed.reshape(flat), induced.reshape(flat))
    return result.reshape((1,) + shape)


def solution(mesh):
    in_specs = (P("inst", None, None, "tile", None), P("inst", None, None, "tile", None))
    out_specs = P("inst", None, None, "tile", None)
    return jax.shard_map(
        per_device, mesh=mesh, in_specs=in_specs, out_specs=out_specs, check_vma=False
    )
```

```python
import functools

import jax
import jax.numpy as jnp
import numpy as np
from jax import lax
from jax.experimental import pallas as pl
from jax.experimental.pallas import tpu as pltpu
from jax.sharding import PartitionSpec as P

RESIST = 0.2
TIME_DAMP = 0.5
LANES = 256
RING = 4
STEPS = ((1, 0), (1, 1), (1, -1), (1, 2), (0, 1), (0, -1), (0, 2))
NEAR = (STEPS[0],) + STEPS[4:]
LAST_ACROSS = ((2, 0, 1, 3), (0, 3, 1, 2), (0, 1, 3, 2), (1, 0, 2, 3))
LAST_BESIDE = ((0, 2), (0, 1), (0, -1))
MESH = pl.DeviceIdType.MESH


def time_weights(count):
    k = np.arange(1, count)
    parity = np.where(k % 2 == 0, 1.0, -1.0)
    sine, cosine = np.sin(np.pi * k / count), np.cos(np.pi * k / count)
    off = 0.5 * parity * cosine / sine + TIME_DAMP * 0.5 * parity / (sine * sine)
    return [TIME_DAMP * (count * count + 2) / 12.0] + [float(v) for v in off]


def mix(fields, weights):
    count = len(fields)
    half = count // 2
    sums = [fields[k] + fields[k + half] for k in range(half)]
    diffs = [fields[k] - fields[k + half] for k in range(half)]

    def dot(terms, row):
        total = None
        for term, weight in zip(terms, row):
            part = term * np.float32(weight)
            total = part if total is None else total + part
        return total

    low, high = [], []
    for q in range(half):
        row = [weights[(q + k) % count] for k in range(half)]
        far = [weights[(q + k + half) % count] for k in range(half)]
        even = dot(sums, [(a + b) / 2 for a, b in zip(row, far)])
        odd = dot(diffs, [(a - b) / 2 for a, b in zip(row, far)])
        low.append(even + odd)
        high.append(even - odd)
    return low + high


def cross(u, b):
    return [u[1] * b[2] - u[2] * b[1], u[2] * b[0] - u[0] * b[2], u[0] * b[1] - u[1] * b[0]]


def x_terms(b, e, sign):
    half = np.float32(0.5 * sign)
    rate = np.float32(RESIST)
    return [rate * b[0], rate * b[1] - half * e[2], rate * b[2] + half * e[1]]


def kernel(weights, b_hbm, u_hbm, mixed, induced, field, flow, emf, got, out, edge, halo,
           load_sem, edge_send, edge_recv, there_send, there_recv, back_send, back_recv, ready):
    count = len(weights)
    comps, planes, rows, lanes = field.shape
    part = rows // count
    me, tile = lax.axis_index("inst"), lax.axis_index("tile")
    tiles = lax.axis_size("tile")
    after, before = lax.rem(tile + 1, tiles), lax.rem(tile + tiles - 1, tiles)

    def moved(step):
        return lax.rem(me // RING + step[0], 2) * RING + lax.rem(me % RING + step[1] + RING, RING)

    def slot(step):
        return lax.rem(moved(step) - me + count, count) - 1

    barrier = pltpu.get_barrier_semaphore()
    for step in NEAR:
        pl.semaphore_signal(barrier, inc=1, device_id=(moved(step), tile), device_id_type=MESH)
    for other in (before, after):
        pl.semaphore_signal(barrier, inc=1, device_id=(me, other), device_id_type=MESH)

    loads = [pltpu.make_async_copy(b_hbm, field, load_sem.at[0]), pltpu.make_async_copy(u_hbm, flow, load_sem.at[1])]
    pl.semaphore_wait(barrier, len(NEAR) + 2)
    pl.semaphore_signal(ready, inc=1, device_id=(moved((1, 0)), tile), device_id_type=MESH)

    def there(z, p):
        step = STEPS[p]
        return pltpu.make_async_remote_copy(
            src_ref=b_hbm.at[:, z, pl.ds(pl.multiple_of(moved(step) * part, part), part), :], dst_ref=got.at[slot(step), z],
            send_sem=there_send.at[z, p], recv_sem=there_recv.at[z, p],
            device_id=(moved(step), tile), device_id_type=MESH)

    own = pl.ds(pl.multiple_of(me * part, part), part)

    def last_step(p):
        if p >= RING:
            return LAST_BESIDE[p - RING]
        spot, place = me % RING, LAST_ACROSS[-1][p]
        for at in range(RING - 1):
            place = jnp.where(spot == at, LAST_ACROSS[at][p], place)
        return (1, place - spot)

    def back(z, p):
        step = last_step(p) if z == planes - 1 else STEPS[p]
        return pltpu.make_async_remote_copy(
            src_ref=out.at[slot(step), z], dst_ref=mixed.at[:, z, own, :],
            send_sem=back_send.at[z, p], recv_sem=back_recv.at[z, slot(step)],
            device_id=(moved(step), tile), device_id_type=MESH)

    for z in range(2):
        for p in (0, 4, 5, 6):
            there(z, p).start()
    pl.semaphore_wait(ready, 1)
    for z in range(2):
        for p in (1, 2, 3):
            there(z, p).start()
    for z in range(2, planes):
        for p in range(len(STEPS)):
            there(z, p).start()

    for load in loads:
        load.start()
    for load in loads:
        load.wait()

    for side, (first, row, sign) in enumerate(((0, 0, 1), (rows - 8, 7, -1))):
        for z in range(planes):
            b = [field[c, z, first:first + 8, :] for c in range(comps)]
            e = cross([flow[c, z, first:first + 8, :] for c in range(comps)], b)
            for c, term in enumerate(x_terms(b, e, sign)):
                at = c * planes + z
                edge[side, at:at + 1, :] = term[row:row + 1, :]

    def edge_copy(side, other):
        return pltpu.make_async_remote_copy(
            src_ref=edge.at[side], dst_ref=halo.at[side], send_sem=edge_send.at[side], recv_sem=edge_recv.at[side],
            device_id=(me, other), device_id_type=MESH)

    edges = [edge_copy(0, before), edge_copy(1, after)]
    for copy in edges:
        copy.start()

    def emf_plane(z, carry):
        b = [field[c, z] for c in range(comps)]
        for c, value in enumerate(cross([flow[c, z] for c in range(comps)], b)):
            emf[c, z] = value
        return carry

    steps = lanes // LANES
    for z in range(planes):
        for p in range(len(STEPS)):
            there(z, p).wait_recv()

        def mix_block(i, carry, z=z):
            c, at = i // steps, pl.ds(pl.multiple_of((i % steps) * LANES, LANES), LANES)
            fields = [field[c, z, own, at]] + [got[k, z, c, :, at] for k in range(count - 1)]
            values = mix(fields, weights)
            mixed[c, z, own, at] = values[0]
            for k in range(1, count):
                out[k - 1, z, c, :, at] = values[k]
            return carry

        lax.fori_loop(0, comps * steps, mix_block, 0)
        for p in range(len(STEPS)):
            back(z, p).start()

    lax.fori_loop(0, planes, emf_plane, 0)

    for copy in edges:
        copy.wait()

    rate, half = np.float32(RESIST), np.float32(0.5)

    def induction_plane(z, carry):
        up, down = lax.rem(z + 1, planes), lax.rem(z + planes - 1, planes)
        b = [field[c, z] for c in range(comps)]
        e = [emf[c, z] for c in range(comps)]
        place = lax.broadcasted_iota(jnp.int32, (rows, lanes), 0)
        from_after, from_before = x_terms(b, e, 1), x_terms(b, e, -1)
        z_emf = [lambda at: -emf[1, at], lambda at: emf[0, at], lambda at: None]
        y_emf = [e[2], None, -e[0]]
        for c in range(comps):
            total = np.float32(-6.0 * RESIST) * b[c]
            total += rate * (field[c, up] + field[c, down])
            if c < 2:
                total += half * (z_emf[c](up) - z_emf[c](down))
            diffusive = rate * b[c]
            ahead, behind = diffusive, diffusive
            if y_emf[c] is not None:
                ahead, behind = diffusive + half * y_emf[c], diffusive - half * y_emf[c]
            total += pltpu.roll(ahead, lanes - 1, 1) + pltpu.roll(behind, 1, 1)
            row = c * planes + z
            next_row, last_row = halo[0, pl.ds(row, 1), :], halo[1, pl.ds(row, 1), :]
            total += jnp.where(place == rows - 1, next_row, pltpu.roll(from_after[c], rows - 1, 0))
            total += jnp.where(place == 0, last_row, pltpu.roll(from_before[c], 1, 0))
            induced[c, z] = total
        return carry

    lax.fori_loop(0, planes, induction_plane, 0)

    for z in range(planes):
        for p in range(len(STEPS)):
            there(z, p).wait_send()
            back(z, p).wait()


def finish(mixed, induced, result, block, sem):
    copies = [pltpu.make_async_copy(block.at[i], result.at[i], sem.at[i]) for i in range(block.shape[0])]
    for i, copy in enumerate(copies):
        block[i] = mixed[i] - induced[i]
        copy.start()
    for copy in copies:
        copy.wait()


def per_device(magnetic, velocity):
    inst_count = lax.axis_size("inst")
    field, flow = (pltpu.with_memory_space_constraint(a[0], pltpu.HBM) for a in (magnetic, velocity))
    shape = field.shape
    comps, planes, rows, lanes = shape
    part = rows // inst_count
    vmem = pl.BlockSpec(memory_space=pltpu.VMEM)
    block = jax.ShapeDtypeStruct(shape, jnp.float32)
    mixed, induced = pl.pallas_call(
        functools.partial(kernel, time_weights(inst_count)),
        out_shape=(block, block),
        in_specs=[pl.BlockSpec(memory_space=pltpu.HBM)] * 2,
        out_specs=(vmem, vmem),
        scratch_shapes=[
            pltpu.VMEM(shape, jnp.float32),
            pltpu.VMEM(shape, jnp.float32),
            pltpu.VMEM(shape, jnp.float32),
            pltpu.VMEM((inst_count - 1, planes, comps, part, lanes), jnp.float32),
            pltpu.VMEM((inst_count - 1, planes, comps, part, lanes), jnp.float32),
            pltpu.VMEM((2, comps * planes, lanes), jnp.float32),
            pltpu.VMEM((2, comps * planes, lanes), jnp.float32),
            pltpu.SemaphoreType.DMA((2,)),
            pltpu.SemaphoreType.DMA((2,)),
            pltpu.SemaphoreType.DMA((2,)),
            pltpu.SemaphoreType.DMA((planes, inst_count - 1)),
            pltpu.SemaphoreType.DMA((planes, inst_count - 1)),
            pltpu.SemaphoreType.DMA((planes, inst_count - 1)),
            pltpu.SemaphoreType.DMA((planes, inst_count - 1)),
            pltpu.SemaphoreType.REGULAR,
        ],
        compiler_params=pltpu.CompilerParams(
            collective_id=0, has_side_effects=True, vmem_limit_bytes=40 * 2**20
        ),
    )(field, flow)
    flat = (comps * planes, rows, lanes)
    result = pl.pallas_call(
        finish,
        out_shape=jax.ShapeDtypeStruct(flat, jnp.float32),
        in_specs=[vmem, vmem],
        out_specs=pl.BlockSpec(memory_space=pltpu.HBM),
        scratch_shapes=[pltpu.VMEM(flat, jnp.float32), pltpu.SemaphoreType.DMA((comps * planes,))],
        compiler_params=pltpu.CompilerParams(vmem_limit_bytes=40 * 2**20),
    )(mixed.reshape(flat), induced.reshape(flat))
    return result.reshape((1,) + shape)


def solution(mesh):
    in_specs = (P("inst", None, None, "tile", None), P("inst", None, None, "tile", None))
    out_specs = P("inst", None, None, "tile", None)
    return jax.shard_map(
        per_device, mesh=mesh, in_specs=in_specs, out_specs=out_specs, check_vma=False
    )
```

```python
import functools

import jax
import jax.numpy as jnp
import numpy as np
from jax import lax
from jax.experimental import pallas as pl
from jax.experimental.pallas import tpu as pltpu
from jax.sharding import PartitionSpec as P

RESIST = 0.2
TIME_DAMP = 0.5
LANES = 256
PIECES = ((0, 2), (2, 1), (3, 1))
EARLY = 1
RING = 4
STEPS = ((1, 0), (1, 1), (1, -1), (1, 2), (0, 1), (0, -1), (0, 2))
NEAR = (STEPS[0],) + STEPS[4:]
LAST_ACROSS = ((2, 0, 1, 3), (0, 3, 1, 2), (0, 1, 3, 2), (1, 0, 2, 3))
LAST_BESIDE = ((0, 2), (0, 1), (0, -1))
MESH = pl.DeviceIdType.MESH


def time_weights(count):
    k = np.arange(1, count)
    parity = np.where(k % 2 == 0, 1.0, -1.0)
    sine, cosine = np.sin(np.pi * k / count), np.cos(np.pi * k / count)
    off = 0.5 * parity * cosine / sine + TIME_DAMP * 0.5 * parity / (sine * sine)
    return [TIME_DAMP * (count * count + 2) / 12.0] + [float(v) for v in off]


def mix(fields, weights):
    count = len(fields)
    half = count // 2
    sums = [fields[k] + fields[k + half] for k in range(half)]
    diffs = [fields[k] - fields[k + half] for k in range(half)]

    def dot(terms, row):
        total = None
        for term, weight in zip(terms, row):
            part = term * np.float32(weight)
            total = part if total is None else total + part
        return total

    low, high = [], []
    for q in range(half):
        row = [weights[(q + k) % count] for k in range(half)]
        far = [weights[(q + k + half) % count] for k in range(half)]
        even = dot(sums, [(a + b) / 2 for a, b in zip(row, far)])
        odd = dot(diffs, [(a - b) / 2 for a, b in zip(row, far)])
        low.append(even + odd)
        high.append(even - odd)
    return low + high


def cross(u, b):
    return [u[1] * b[2] - u[2] * b[1], u[2] * b[0] - u[0] * b[2], u[0] * b[1] - u[1] * b[0]]


def x_terms(b, e, sign):
    half = np.float32(0.5 * sign)
    rate = np.float32(RESIST)
    return [rate * b[0], rate * b[1] - half * e[2], rate * b[2] + half * e[1]]


def kernel(weights, b_hbm, u_hbm, mixed, induced, field, flow, emf, got, out, edge, halo,
           load_sem, edge_send, edge_recv, there_send, there_recv, back_send, back_recv, ready):
    count = len(weights)
    comps, planes, rows, lanes = field.shape
    part = rows // count
    me, tile = lax.axis_index("inst"), lax.axis_index("tile")
    tiles = lax.axis_size("tile")
    after, before = lax.rem(tile + 1, tiles), lax.rem(tile + tiles - 1, tiles)

    def moved(step):
        return lax.rem(me // RING + step[0], 2) * RING + lax.rem(me % RING + step[1] + RING, RING)

    def slot(step):
        return lax.rem(moved(step) - me + count, count) - 1

    barrier = pltpu.get_barrier_semaphore()
    for step in NEAR:
        pl.semaphore_signal(barrier, inc=1, device_id=(moved(step), tile), device_id_type=MESH)
    for other in (before, after):
        pl.semaphore_signal(barrier, inc=1, device_id=(me, other), device_id_type=MESH)

    loads = [pltpu.make_async_copy(b_hbm, field, load_sem.at[0]), pltpu.make_async_copy(u_hbm, flow, load_sem.at[1])]
    pl.semaphore_wait(barrier, len(NEAR) + 2)
    pl.semaphore_signal(ready, inc=1, device_id=(moved((1, 0)), tile), device_id_type=MESH)

    def there(q, p):
        step, at = STEPS[p], pl.ds(*PIECES[q])
        return pltpu.make_async_remote_copy(
            src_ref=b_hbm.at[:, at, pl.ds(pl.multiple_of(moved(step) * part, part), part), :], dst_ref=got.at[slot(step), :, at],
            send_sem=there_send.at[q, p], recv_sem=there_recv.at[q, p],
            device_id=(moved(step), tile), device_id_type=MESH)

    own = pl.ds(pl.multiple_of(me * part, part), part)

    def last_step(p):
        if p >= RING:
            return LAST_BESIDE[p - RING]
        spot, place = me % RING, LAST_ACROSS[-1][p]
        for at in range(RING - 1):
            place = jnp.where(spot == at, LAST_ACROSS[at][p], place)
        return (1, place - spot)

    def back(q, p):
        step, at = last_step(p) if q == len(PIECES) - 1 else STEPS[p], pl.ds(*PIECES[q])
        return pltpu.make_async_remote_copy(
            src_ref=out.at[slot(step), :, at], dst_ref=mixed.at[:, at, own, :],
            send_sem=back_send.at[q, p], recv_sem=back_recv.at[q, slot(step)],
            device_id=(moved(step), tile), device_id_type=MESH)

    for q in range(EARLY):
        for p in (0, 4, 5, 6):
            there(q, p).start()
    pl.semaphore_wait(ready, 1)
    for q in range(EARLY):
        for p in (1, 2, 3):
            there(q, p).start()
    for q in range(EARLY, len(PIECES)):
        for p in range(len(STEPS)):
            there(q, p).start()

    for load in loads:
        load.start()
    for load in loads:
        load.wait()

    for side, (first, row, sign) in enumerate(((0, 0, 1), (rows - 8, 7, -1))):
        for z in range(planes):
            b = [field[c, z, first:first + 8, :] for c in range(comps)]
            e = cross([flow[c, z, first:first + 8, :] for c in range(comps)], b)
            for c, term in enumerate(x_terms(b, e, sign)):
                at = c * planes + z
                edge[side, at:at + 1, :] = term[row:row + 1, :]

    def edge_copy(side, other):
        return pltpu.make_async_remote_copy(
            src_ref=edge.at[side], dst_ref=halo.at[side], send_sem=edge_send.at[side], recv_sem=edge_recv.at[side],
            device_id=(me, other), device_id_type=MESH)

    edges = [edge_copy(0, before), edge_copy(1, after)]
    for copy in edges:
        copy.start()

    def emf_plane(z, carry):
        b = [field[c, z] for c in range(comps)]
        for c, value in enumerate(cross([flow[c, z] for c in range(comps)], b)):
            emf[c, z] = value
        return carry

    steps = lanes // LANES
    for q, (first, depth) in enumerate(PIECES):
        for p in range(len(STEPS)):
            there(q, p).wait_recv()

        def mix_block(i, carry, first=first):
            z, c, at = first + i // (comps * steps), i // steps % comps, pl.ds(pl.multiple_of((i % steps) * LANES, LANES), LANES)
            fields = [field[c, z, own, at]] + [got[k, c, z, :, at] for k in range(count - 1)]
            values = mix(fields, weights)
            mixed[c, z, own, at] = values[0]
            for k in range(1, count):
                out[k - 1, c, z, :, at] = values[k]
            return carry

        lax.fori_loop(0, depth * comps * steps, mix_block, 0)
        for p in range(len(STEPS)):
            back(q, p).start()

    lax.fori_loop(0, planes, emf_plane, 0)

    for copy in edges:
        copy.wait()

    rate, half = np.float32(RESIST), np.float32(0.5)

    def induction_plane(z, carry):
        up, down = lax.rem(z + 1, planes), lax.rem(z + planes - 1, planes)
        b = [field[c, z] for c in range(comps)]
        e = [emf[c, z] for c in range(comps)]
        place = lax.broadcasted_iota(jnp.int32, (rows, lanes), 0)
        from_after, from_before = x_terms(b, e, 1), x_terms(b, e, -1)
        z_emf = [lambda at: -emf[1, at], lambda at: emf[0, at], lambda at: None]
        y_emf = [e[2], None, -e[0]]
        for c in range(comps):
            total = np.float32(-6.0 * RESIST) * b[c]
            total += rate * (field[c, up] + field[c, down])
            if c < 2:
                total += half * (z_emf[c](up) - z_emf[c](down))
            diffusive = rate * b[c]
            ahead, behind = diffusive, diffusive
            if y_emf[c] is not None:
                ahead, behind = diffusive + half * y_emf[c], diffusive - half * y_emf[c]
            total += pltpu.roll(ahead, lanes - 1, 1) + pltpu.roll(behind, 1, 1)
            row = c * planes + z
            next_row, last_row = halo[0, pl.ds(row, 1), :], halo[1, pl.ds(row, 1), :]
            total += jnp.where(place == rows - 1, next_row, pltpu.roll(from_after[c], rows - 1, 0))
            total += jnp.where(place == 0, last_row, pltpu.roll(from_before[c], 1, 0))
            induced[c, z] = total
        return carry

    lax.fori_loop(0, planes, induction_plane, 0)

    for q in range(len(PIECES)):
        for p in range(len(STEPS)):
            there(q, p).wait_send()
            back(q, p).wait()


def finish(mixed, induced, result, block, sem):
    copies = [pltpu.make_async_copy(block.at[i], result.at[i], sem.at[i]) for i in range(block.shape[0])]
    for i, copy in enumerate(copies):
        block[i] = mixed[i] - induced[i]
        copy.start()
    for copy in copies:
        copy.wait()


def per_device(magnetic, velocity):
    inst_count = lax.axis_size("inst")
    field, flow = (pltpu.with_memory_space_constraint(a[0], pltpu.HBM) for a in (magnetic, velocity))
    shape = field.shape
    comps, planes, rows, lanes = shape
    part = rows // inst_count
    vmem = pl.BlockSpec(memory_space=pltpu.VMEM)
    block = jax.ShapeDtypeStruct(shape, jnp.float32)
    mixed, induced = pl.pallas_call(
        functools.partial(kernel, time_weights(inst_count)),
        out_shape=(block, block),
        in_specs=[pl.BlockSpec(memory_space=pltpu.HBM)] * 2,
        out_specs=(vmem, vmem),
        scratch_shapes=[
            pltpu.VMEM(shape, jnp.float32),
            pltpu.VMEM(shape, jnp.float32),
            pltpu.VMEM(shape, jnp.float32),
            pltpu.VMEM((inst_count - 1, comps, planes, part, lanes), jnp.float32),
            pltpu.VMEM((inst_count - 1, comps, planes, part, lanes), jnp.float32),
            pltpu.VMEM((2, comps * planes, lanes), jnp.float32),
            pltpu.VMEM((2, comps * planes, lanes), jnp.float32),
            pltpu.SemaphoreType.DMA((2,)),
            pltpu.SemaphoreType.DMA((2,)),
            pltpu.SemaphoreType.DMA((2,)),
            pltpu.SemaphoreType.DMA((len(PIECES), inst_count - 1)),
            pltpu.SemaphoreType.DMA((len(PIECES), inst_count - 1)),
            pltpu.SemaphoreType.DMA((len(PIECES), inst_count - 1)),
            pltpu.SemaphoreType.DMA((len(PIECES), inst_count - 1)),
            pltpu.SemaphoreType.REGULAR,
        ],
        compiler_params=pltpu.CompilerParams(
            collective_id=0, has_side_effects=True, vmem_limit_bytes=40 * 2**20
        ),
    )(field, flow)
    flat = (comps * planes, rows, lanes)
    result = pl.pallas_call(
        finish,
        out_shape=jax.ShapeDtypeStruct(flat, jnp.float32),
        in_specs=[vmem, vmem],
        out_specs=pl.BlockSpec(memory_space=pltpu.HBM),
        scratch_shapes=[pltpu.VMEM(flat, jnp.float32), pltpu.SemaphoreType.DMA((comps * planes,))],
        compiler_params=pltpu.CompilerParams(vmem_limit_bytes=40 * 2**20),
    )(mixed.reshape(flat), induced.reshape(flat))
    return result.reshape((1,) + shape)


def solution(mesh):
    in_specs = (P("inst", None, None, "tile", None), P("inst", None, None, "tile", None))
    out_specs = P("inst", None, None, "tile", None)
    return jax.shard_map(
        per_device, mesh=mesh, in_specs=in_specs, out_specs=out_specs, check_vma=False
    )
```

```python
import functools

import jax
import jax.numpy as jnp
import numpy as np
from jax import lax
from jax.experimental import pallas as pl
from jax.experimental.pallas import tpu as pltpu
from jax.sharding import PartitionSpec as P

RESIST = 0.2
TIME_DAMP = 0.5
LANES = 256
PIECES = ((0, 1), (1, 2), (3, 1))
EARLY = 1
RING = 4
STEPS = ((1, 0), (1, 1), (1, -1), (1, 2), (0, 1), (0, -1), (0, 2))
NEAR = (STEPS[0],) + STEPS[4:]
LAST_ACROSS = ((2, 0, 1, 3), (0, 3, 1, 2), (0, 1, 3, 2), (1, 0, 2, 3))
LAST_BESIDE = ((0, 2), (0, 1), (0, -1))
MESH = pl.DeviceIdType.MESH


def time_weights(count):
    k = np.arange(1, count)
    parity = np.where(k % 2 == 0, 1.0, -1.0)
    sine, cosine = np.sin(np.pi * k / count), np.cos(np.pi * k / count)
    off = 0.5 * parity * cosine / sine + TIME_DAMP * 0.5 * parity / (sine * sine)
    return [TIME_DAMP * (count * count + 2) / 12.0] + [float(v) for v in off]


def mix(fields, weights):
    count = len(fields)
    half = count // 2
    sums = [fields[k] + fields[k + half] for k in range(half)]
    diffs = [fields[k] - fields[k + half] for k in range(half)]

    def dot(terms, row):
        total = None
        for term, weight in zip(terms, row):
            part = term * np.float32(weight)
            total = part if total is None else total + part
        return total

    low, high = [], []
    for q in range(half):
        row = [weights[(q + k) % count] for k in range(half)]
        far = [weights[(q + k + half) % count] for k in range(half)]
        even = dot(sums, [(a + b) / 2 for a, b in zip(row, far)])
        odd = dot(diffs, [(a - b) / 2 for a, b in zip(row, far)])
        low.append(even + odd)
        high.append(even - odd)
    return low + high


def cross(u, b):
    return [u[1] * b[2] - u[2] * b[1], u[2] * b[0] - u[0] * b[2], u[0] * b[1] - u[1] * b[0]]


def x_terms(b, e, sign):
    half = np.float32(0.5 * sign)
    rate = np.float32(RESIST)
    return [rate * b[0], rate * b[1] - half * e[2], rate * b[2] + half * e[1]]


def kernel(weights, b_hbm, u_hbm, mixed, induced, field, flow, emf, got, out, edge, halo,
           load_sem, edge_send, edge_recv, there_send, there_recv, back_send, back_recv, ready):
    count = len(weights)
    comps, planes, rows, lanes = field.shape
    part = rows // count
    me, tile = lax.axis_index("inst"), lax.axis_index("tile")
    tiles = lax.axis_size("tile")
    after, before = lax.rem(tile + 1, tiles), lax.rem(tile + tiles - 1, tiles)

    def moved(step):
        return lax.rem(me // RING + step[0], 2) * RING + lax.rem(me % RING + step[1] + RING, RING)

    def slot(step):
        return lax.rem(moved(step) - me + count, count) - 1

    barrier = pltpu.get_barrier_semaphore()
    for step in NEAR:
        pl.semaphore_signal(barrier, inc=1, device_id=(moved(step), tile), device_id_type=MESH)
    for other in (before, after):
        pl.semaphore_signal(barrier, inc=1, device_id=(me, other), device_id_type=MESH)

    loads = [pltpu.make_async_copy(b_hbm, field, load_sem.at[0]), pltpu.make_async_copy(u_hbm, flow, load_sem.at[1])]
    pl.semaphore_wait(barrier, len(NEAR) + 2)
    pl.semaphore_signal(ready, inc=1, device_id=(moved((1, 0)), tile), device_id_type=MESH)

    def there(q, p):
        step, at = STEPS[p], pl.ds(*PIECES[q])
        return pltpu.make_async_remote_copy(
            src_ref=b_hbm.at[:, at, pl.ds(pl.multiple_of(moved(step) * part, part), part), :], dst_ref=got.at[slot(step), :, at],
            send_sem=there_send.at[q, p], recv_sem=there_recv.at[q, p],
            device_id=(moved(step), tile), device_id_type=MESH)

    own = pl.ds(pl.multiple_of(me * part, part), part)

    def last_step(p):
        if p >= RING:
            return LAST_BESIDE[p - RING]
        spot, place = me % RING, LAST_ACROSS[-1][p]
        for at in range(RING - 1):
            place = jnp.where(spot == at, LAST_ACROSS[at][p], place)
        return (1, place - spot)

    def back(q, p):
        step, at = last_step(p) if q == len(PIECES) - 1 else STEPS[p], pl.ds(*PIECES[q])
        return pltpu.make_async_remote_copy(
            src_ref=out.at[slot(step), :, at], dst_ref=mixed.at[:, at, own, :],
            send_sem=back_send.at[q, p], recv_sem=back_recv.at[q, slot(step)],
            device_id=(moved(step), tile), device_id_type=MESH)

    for q in range(EARLY):
        for p in (0, 4, 5, 6):
            there(q, p).start()
    pl.semaphore_wait(ready, 1)
    for q in range(EARLY):
        for p in (1, 2, 3):
            there(q, p).start()
    for q in range(EARLY, len(PIECES)):
        for p in range(len(STEPS)):
            there(q, p).start()

    for load in loads:
        load.start()
    for load in loads:
        load.wait()

    for side, (first, row, sign) in enumerate(((0, 0, 1), (rows - 8, 7, -1))):
        for z in range(planes):
            b = [field[c, z, first:first + 8, :] for c in range(comps)]
            e = cross([flow[c, z, first:first + 8, :] for c in range(comps)], b)
            for c, term in enumerate(x_terms(b, e, sign)):
                at = c * planes + z
                edge[side, at:at + 1, :] = term[row:row + 1, :]

    def edge_copy(side, other):
        return pltpu.make_async_remote_copy(
            src_ref=edge.at[side], dst_ref=halo.at[side], send_sem=edge_send.at[side], recv_sem=edge_recv.at[side],
            device_id=(me, other), device_id_type=MESH)

    edges = [edge_copy(0, before), edge_copy(1, after)]
    for copy in edges:
        copy.start()

    def emf_plane(z, carry):
        b = [field[c, z] for c in range(comps)]
        for c, value in enumerate(cross([flow[c, z] for c in range(comps)], b)):
            emf[c, z] = value
        return carry

    steps = lanes // LANES
    for q, (first, depth) in enumerate(PIECES):
        for p in range(len(STEPS)):
            there(q, p).wait_recv()

        def mix_block(i, carry, first=first):
            z, c, at = first + i // (comps * steps), i // steps % comps, pl.ds(pl.multiple_of((i % steps) * LANES, LANES), LANES)
            fields = [field[c, z, own, at]] + [got[k, c, z, :, at] for k in range(count - 1)]
            values = mix(fields, weights)
            mixed[c, z, own, at] = values[0]
            for k in range(1, count):
                out[k - 1, c, z, :, at] = values[k]
            return carry

        lax.fori_loop(0, depth * comps * steps, mix_block, 0)
        for p in range(len(STEPS)):
            back(q, p).start()

    lax.fori_loop(0, planes, emf_plane, 0)

    for copy in edges:
        copy.wait()

    rate, half = np.float32(RESIST), np.float32(0.5)

    def induction_plane(z, carry):
        up, down = lax.rem(z + 1, planes), lax.rem(z + planes - 1, planes)
        b = [field[c, z] for c in range(comps)]
        e = [emf[c, z] for c in range(comps)]
        place = lax.broadcasted_iota(jnp.int32, (rows, lanes), 0)
        from_after, from_before = x_terms(b, e, 1), x_terms(b, e, -1)
        z_emf = [lambda at: -emf[1, at], lambda at: emf[0, at], lambda at: None]
        y_emf = [e[2], None, -e[0]]
        for c in range(comps):
            total = np.float32(-6.0 * RESIST) * b[c]
            total += rate * (field[c, up] + field[c, down])
            if c < 2:
                total += half * (z_emf[c](up) - z_emf[c](down))
            diffusive = rate * b[c]
            ahead, behind = diffusive, diffusive
            if y_emf[c] is not None:
                ahead, behind = diffusive + half * y_emf[c], diffusive - half * y_emf[c]
            total += pltpu.roll(ahead, lanes - 1, 1) + pltpu.roll(behind, 1, 1)
            row = c * planes + z
            next_row, last_row = halo[0, pl.ds(row, 1), :], halo[1, pl.ds(row, 1), :]
            total += jnp.where(place == rows - 1, next_row, pltpu.roll(from_after[c], rows - 1, 0))
            total += jnp.where(place == 0, last_row, pltpu.roll(from_before[c], 1, 0))
            induced[c, z] = total
        return carry

    lax.fori_loop(0, planes, induction_plane, 0)

    for q in range(len(PIECES)):
        for p in range(len(STEPS)):
            there(q, p).wait_send()
            back(q, p).wait()


def finish(mixed, induced, result, block, sem):
    copies = [pltpu.make_async_copy(block.at[i], result.at[i], sem.at[i]) for i in range(block.shape[0])]
    for i, copy in enumerate(copies):
        block[i] = mixed[i] - induced[i]
        copy.start()
    for copy in copies:
        copy.wait()


def per_device(magnetic, velocity):
    inst_count = lax.axis_size("inst")
    field, flow = (pltpu.with_memory_space_constraint(a[0], pltpu.HBM) for a in (magnetic, velocity))
    shape = field.shape
    comps, planes, rows, lanes = shape
    part = rows // inst_count
    vmem = pl.BlockSpec(memory_space=pltpu.VMEM)
    block = jax.ShapeDtypeStruct(shape, jnp.float32)
    mixed, induced = pl.pallas_call(
        functools.partial(kernel, time_weights(inst_count)),
        out_shape=(block, block),
        in_specs=[pl.BlockSpec(memory_space=pltpu.HBM)] * 2,
        out_specs=(vmem, vmem),
        scratch_shapes=[
            pltpu.VMEM(shape, jnp.float32),
            pltpu.VMEM(shape, jnp.float32),
            pltpu.VMEM(shape, jnp.float32),
            pltpu.VMEM((inst_count - 1, comps, planes, part, lanes), jnp.float32),
            pltpu.VMEM((inst_count - 1, comps, planes, part, lanes), jnp.float32),
            pltpu.VMEM((2, comps * planes, lanes), jnp.float32),
            pltpu.VMEM((2, comps * planes, lanes), jnp.float32),
            pltpu.SemaphoreType.DMA((2,)),
            pltpu.SemaphoreType.DMA((2,)),
            pltpu.SemaphoreType.DMA((2,)),
            pltpu.SemaphoreType.DMA((len(PIECES), inst_count - 1)),
            pltpu.SemaphoreType.DMA((len(PIECES), inst_count - 1)),
            pltpu.SemaphoreType.DMA((len(PIECES), inst_count - 1)),
            pltpu.SemaphoreType.DMA((len(PIECES), inst_count - 1)),
            pltpu.SemaphoreType.REGULAR,
        ],
        compiler_params=pltpu.CompilerParams(
            collective_id=0, has_side_effects=True, vmem_limit_bytes=40 * 2**20
        ),
    )(field, flow)
    flat = (comps * planes, rows, lanes)
    result = pl.pallas_call(
        finish,
        out_shape=jax.ShapeDtypeStruct(flat, jnp.float32),
        in_specs=[vmem, vmem],
        out_specs=pl.BlockSpec(memory_space=pltpu.HBM),
        scratch_shapes=[pltpu.VMEM(flat, jnp.float32), pltpu.SemaphoreType.DMA((comps * planes,))],
        compiler_params=pltpu.CompilerParams(vmem_limit_bytes=40 * 2**20),
    )(mixed.reshape(flat), induced.reshape(flat))
    return result.reshape((1,) + shape)


def solution(mesh):
    in_specs = (P("inst", None, None, "tile", None), P("inst", None, None, "tile", None))
    out_specs = P("inst", None, None, "tile", None)
    return jax.shard_map(
        per_device, mesh=mesh, in_specs=in_specs, out_specs=out_specs, check_vma=False
    )
```
